32 devices in a mesh: dp: 2 (over x), context: 4 (over y, core), expert: 4 (over z).
Axes of the slice: x: 2, y: 2, z: 4, core: 2. Of those that a mesh axis runs over, the one named last changes fastest.
Arguments:
- tokens: bfloat16 [8, 1024, 768], P(('dp', 'expert'), 'context'), may hold values from -6 to 6
- norm1_gain: float32 [768], replicated, may hold values from 0.1 to 1.9
- w_qkv: bfloat16 [768, 2304], replicated, may hold values from -0.21875 to 0.21875
- w_out: bfloat16 [768, 768], replicated, may hold values from -1.75 to 1.75
- bias_table: float32 [32, 12], replicated, may hold values from -4 to 4
- norm2_gain: float32 [768], replicated, may hold values from 0.1 to 1.9
- router: float32 [768, 4], replicated, may hold values from -0.2 to 0.2
- expert_in: bfloat16 [4, 768, 3072], P('expert'), may hold values from -0.21875 to 0.21875
- expert_out: bfloat16 [4, 3072, 768], P('expert'), may hold values from -0.75 to 0.75
- route: int32 [8, 1024], P(('dp', 'expert'), 'context'), may hold values from 0 to 3, as said below
- slot: int32 [8, 1024], P(('dp', 'expert'), 'context'), may hold values from -1 to 79, as said below
- cotangent: bfloat16 [8, 1024, 768], P(('dp', 'expert'), 'context'), may hold values from -6 to 6
Outputs:
- layer_out: bfloat16 [8, 1024, 768], P(('dp', 'expert'), 'context')
- input_grad: bfloat16 [8, 1024, 768], P(('dp', 'expert'), 'context')
- grad_norm1: float32 [768], replicated
- grad_qkv: float32 [768, 2304], P(('dp', 'context'), 'expert')
- grad_wout: float32 [768, 768], P(('dp', 'context'), 'expert')
- grad_bias: float32 [32, 12], replicated
- grad_norm2: float32 [768], replicated
- grad_router: float32 [768, 4], replicated
- grad_expert_in: float32 [4, 768, 3072], P('expert', None, ('dp', 'context'))
- grad_expert_out: float32 [4, 3072, 768], P('expert', ('dp', 'context'))
The draws below stay inside these ranges and needn't reach their ends.
Inputs may be any that keep to these rules, and one draw needn't show every extreme that they name: `route`: the expert that each token is sent to. `slot`: counted over the rows of one device (its sequences in order, then positions), the tokens sent to one expert hold slots 0, 1, 2, ... in that order up to 79; later ones are dropped and hold -1. In every draw some expert is sent more than 80 tokens of some device, and for each index of dp and of context one expert gets all its 80 slots filled from every device of the expert axis.
All inputs are finite; a program needn't handle non-finite values.
Results may differ from the reference program's by a relative error of at most 0.02.
Values may be sent and summed in bfloat16 or wider, within the bound.
A program may use at most 192 MiB of HBM per device.

```python
import math
from functools import partial
import jax
import jax.numpy as jnp
from jax import lax

D = 768
HEADS = 12
HEAD_DIM = 64
FF = 3072
BUCKETS = 32
SEQS = 1
SEQ_DEV = 256
LENGTH = 1024
SEQUENCES = 8
EXPERTS = 4
CAP = 80
N_CONTEXT = 4


def shuffled(single_key):
    return jax.random.permutation(single_key, SEQS * SEQ_DEV)


def route_and_slot(key):
    groups = SEQUENCES // SEQS
    columns = LENGTH // SEQ_DEV
    rows_each = SEQS * SEQ_DEV
    base_key, hot_key, order_key = jax.random.split(key, 3)
    routes = jax.random.randint(base_key, (groups, columns, rows_each), 0, EXPERTS)
    replicas = groups // EXPERTS
    hot_expert = jax.random.randint(hot_key, (replicas, 1, columns, 1), 0, EXPERTS)
    hot_expert = jnp.broadcast_to(hot_expert, (replicas, EXPERTS, columns, rows_each)).reshape(groups, columns, rows_each)
    order_keys = jax.random.split(order_key, groups * columns)
    orders = jax.vmap(shuffled)(order_keys).reshape(groups, columns, rows_each)
    routes = jnp.where(orders < CAP + CAP // 2, hot_expert, routes).astype(jnp.int32)
    onehot = (routes[..., None] == jnp.arange(EXPERTS, dtype=jnp.int32)).astype(jnp.int32)
    ranks = jnp.cumsum(onehot, axis=2) - 1
    slots = jnp.sum(ranks * onehot, axis=3)
    slots = jnp.where(slots < CAP, slots, -1).astype(jnp.int32)

    def layout(values):
        return jnp.transpose(values.reshape(groups, columns, SEQS, SEQ_DEV), (0, 2, 1, 3)).reshape(SEQUENCES, LENGTH)
    return (layout(routes), layout(slots))


def draw_route(key, part):
    shared = route_and_slot(key)
    return shared[0]


def draw_slot(key, part):
    shared = route_and_slot(key)
    return shared[1]


def levels(own_key, shape, pieces, least, high):
    level, own = 1.0, jax.random.fold_in(own_key, 6)
    for axis_at, shards_of in pieces:
        steps = jnp.exp(jax.random.uniform(jax.random.fold_in(own, axis_at), (shards_of,), jnp.float32, least / len(pieces), high / len(pieces)))
        level = level * jnp.repeat(steps, shape[axis_at] // shards_of).reshape([-1 if axis == axis_at else 1 for axis in range(len(shape))])
    return level


def noise(stream_key, extent, deviation, bound, cuts=(), held_as=jnp.bfloat16):
    factor_of = levels(stream_key, extent, cuts, -0.22, 0.18) if cuts else 1.0
    values = jax.random.normal(stream_key, extent, jnp.float32) * deviation * factor_of
    return jnp.minimum(jnp.maximum(values, -bound), bound).astype(held_as)


def setup_inputs(seed: int = 0) -> dict:
    key_list = jax.random.split(jax.random.key(seed), 13)
    return {
        "tokens": noise(key_list[0], (SEQUENCES, LENGTH, D), 1.0, 6.0, ((0, 8), (1, 4))),
        "norm1_gain": jnp.clip(1.0 + 0.18 * jax.random.normal(key_list[1], (D,), jnp.float32), 0.1, 1.9),
        "w_qkv": noise(key_list[2], (D, 3 * D), D ** -0.5, 0.21875),
        "w_out": noise(key_list[3], (D, D), (D // 64) ** -0.5, 1.75),
        "bias_table": noise(key_list[4], (BUCKETS, HEADS), 1.0, 4.0, (), jnp.float32),
        "norm2_gain": jnp.clip(1.0 + 0.18 * jax.random.normal(key_list[5], (D,), jnp.float32), 0.1, 1.9),
        "router": noise(key_list[6], (D, EXPERTS), 0.027, 0.2, (), jnp.float32),
        "expert_in": noise(key_list[7], (EXPERTS, D, FF), D ** -0.5, 0.21875, ((0, 4),)),
        "expert_out": noise(key_list[8], (EXPERTS, FF, D), (max(1, 1024 // (EXPERTS * EXPERTS))) ** -0.5, 0.75, ((0, 4),)),
        "route": draw_route(jax.random.fold_in(key_list[12], 71), 0),
        "slot": draw_slot(jax.random.fold_in(key_list[12], 71), 0),
        "cotangent": noise(key_list[11], (SEQUENCES, LENGTH, D), 1.0, 6.0, ((0, 8), (1, 4))),
    }


@jax.custom_vjp
def low(v):
    return lax.optimization_barrier(v.astype(jnp.bfloat16)).astype(jnp.float32)

@jax.custom_vjp
def low_back(v):
    return v

def low_keep(v):
    return (low(v), None)

def low_pass(kept, grad):
    return (grad,)

def back_keep(v):
    return (v, None)

def back_low(kept, grad):
    return (low(grad),)
low.defvjp(low_keep, low_pass)
low_back.defvjp(back_keep, back_low)
THRESHOLDS = (12, 16, 23, 32, 46, 64, 91)
SCORE_SCALE = 0.125
EPSILON = 1e-06
HIGHEST = lax.Precision.HIGHEST

def bucket_index(relative):
    distance = jnp.abs(relative)
    far_level = jnp.full_like(distance, 8)
    for threshold in THRESHOLDS:
        far_level = far_level + (distance >= threshold).astype(jnp.int32)
    near_far = jnp.where(distance < 8, distance, far_level)
    return near_far + 16 * (relative > 0).astype(jnp.int32)

def rms_norm(values, gain):
    return values * lax.rsqrt(lax.optimization_barrier(jnp.mean(values * values, axis=-1, keepdims=True)) + EPSILON) * gain

def attend_group(group, bias_table):
    queries, keys, values = group
    block_rows = math.gcd(LENGTH, 1024)
    blocks = LENGTH // block_rows
    query_blocks = jnp.transpose(queries.reshape(SEQS, blocks, block_rows, HEADS, HEAD_DIM), (1, 0, 2, 3, 4))
    starts = jnp.arange(blocks, dtype=jnp.int32) * block_rows

    def one_block(packed):
        query_block, start = packed
        query_pos = start + jnp.arange(block_rows, dtype=jnp.int32)
        key_pos = jnp.arange(LENGTH, dtype=jnp.int32)
        buckets = bucket_index(key_pos[None, :] - query_pos[:, None])
        position_bias = jnp.transpose(jnp.take(bias_table, buckets, axis=0), (2, 0, 1))
        scores = jnp.einsum('sqhd,skhd->shqk', query_block, keys, precision=HIGHEST) * SCORE_SCALE + position_bias[None]
        scores = low_back(scores)
        probs = low(jax.nn.softmax(scores, axis=-1))
        return jnp.einsum('shqk,skhd->sqhd', probs, values, precision=HIGHEST)
    produced = lax.map(jax.checkpoint(one_block), (query_blocks, starts))
    return jnp.transpose(produced, (1, 0, 2, 3, 4)).reshape(SEQS, LENGTH, HEADS, HEAD_DIM)

def run_expert(packed):
    rows, weight_in, weight_out = packed
    pre_act = low_back(jnp.dot(rows, weight_in, precision=HIGHEST))
    activated = low(jax.nn.gelu(pre_act, approximate=True))
    return low_back(low(jnp.dot(activated, weight_out, precision=HIGHEST)))

def forward(inputs, norm1_gain, w_qkv, w_out, bias_table, norm2_gain, router, expert_in, expert_out, route, slot):
    groups = SEQUENCES // SEQS
    flat_inputs = inputs.reshape(SEQUENCES * LENGTH, D)
    normed_one = low(rms_norm(flat_inputs, norm1_gain))
    projected = low(jnp.dot(normed_one, w_qkv, precision=HIGHEST))
    shape_heads = (groups, SEQS, LENGTH, HEADS, HEAD_DIM)
    queries = low_back(projected[:, :D]).reshape(shape_heads)
    keys = low_back(projected[:, D:2 * D]).reshape(shape_heads)
    values = low_back(projected[:, 2 * D:]).reshape(shape_heads)
    attended = lax.map(partial(attend_group, bias_table=bias_table), (queries, keys, values))
    attended = low_back(low(attended.reshape(SEQUENCES * LENGTH, D)))
    branch = low_back(jnp.dot(attended, w_out, precision=HIGHEST))
    hidden_sum = flat_inputs + branch
    normed_two = rms_norm(hidden_sum, norm2_gain)
    gates_all = jax.nn.softmax(jnp.dot(normed_two, router, precision=HIGHEST), axis=-1)
    routes = route.reshape(-1).astype(jnp.int32)
    slots = slot.reshape(-1).astype(jnp.int32)
    gate = jnp.take_along_axis(gates_all, routes[:, None], axis=1)[:, 0]
    sent = low_back(low(normed_two))
    seq_ids = jnp.arange(SEQUENCES, dtype=jnp.int32)[:, None]
    pos_ids = jnp.arange(LENGTH, dtype=jnp.int32)[None, :]
    block_ids = (seq_ids // SEQS * N_CONTEXT + pos_ids // SEQ_DEV).reshape(-1)
    blocks_total = groups * N_CONTEXT
    flat_index = jnp.where(slots >= 0, (block_ids * EXPERTS + routes) * CAP + slots, blocks_total * EXPERTS * CAP).astype(jnp.int32)
    buffer = jnp.zeros((blocks_total * EXPERTS * CAP, D), jnp.float32).at[flat_index].set(sent, mode='drop')
    by_expert = jnp.transpose(buffer.reshape(blocks_total, EXPERTS, CAP, D), (1, 0, 2, 3)).reshape(EXPERTS, blocks_total * CAP, D)
    produced = lax.map(jax.checkpoint(run_expert), (by_expert, expert_in, expert_out))
    returned = jnp.transpose(produced.reshape(EXPERTS, blocks_total, CAP, D), (1, 0, 2, 3)).reshape(-1, D)
    expert_rows = jnp.take(returned, flat_index, axis=0, mode='fill', fill_value=0.0)
    return (hidden_sum + gate[:, None] * expert_rows).reshape(SEQUENCES, LENGTH, D)

def reference(tokens, norm1_gain, w_qkv, w_out, bias_table, norm2_gain, router, expert_in, expert_out, route, slot, cotangent):
    floats = (tokens.astype(jnp.float32), norm1_gain.astype(jnp.float32), w_qkv.astype(jnp.float32), w_out.astype(jnp.float32), bias_table.astype(jnp.float32), norm2_gain.astype(jnp.float32), router.astype(jnp.float32), expert_in.astype(jnp.float32), expert_out.astype(jnp.float32))
    layer_rows, pullback = jax.vjp(partial(forward, route=route, slot=slot), *floats)
    grads = pullback(cotangent.astype(jnp.float32))
    return (layer_rows.astype(jnp.bfloat16), grads[0].astype(jnp.bfloat16), grads[1], grads[2], grads[3], grads[4], grads[5], grads[6], grads[7], grads[8])
```

```python
import jax
import jax.numpy as jnp
from jax import lax
from jax.experimental import pallas as pl
from jax.experimental.pallas import tpu as pltpu
from jax.sharding import PartitionSpec as P

D = 768
HEADS = 12
HEAD_DIM = 64
BUCKETS = 32


THRESHOLDS = (12, 16, 23, 32, 46, 64, 91)
SCORE_SCALE = 0.125
EPSILON = 1e-06
HIGHEST = lax.Precision.HIGHEST


def bucket_index(relative):
    distance = jnp.abs(relative)
    far_level = jnp.full_like(distance, 8)
    for threshold in THRESHOLDS:
        far_level = far_level + (distance >= threshold).astype(jnp.int32)
    near_far = jnp.where(distance < 8, distance, far_level)
    return near_far + 16 * (relative > 0).astype(jnp.int32)


def norm_back(grad_normed, values, inverse, gain):
    scaled_grad = grad_normed * gain
    grad_gain = jnp.sum(grad_normed * values * inverse, axis=0)
    grad_values = inverse * scaled_grad - values * inverse**3 * jnp.mean(
        scaled_grad * values, axis=1, keepdims=True
    )
    return (grad_gain, grad_values)


PAIR = 2 * HEAD_DIM
PAIRS = HEADS // 2
GELU_ROOT = 0.7978845608028654
GELU_CUBE = 0.044715


def lane_dot(left, right, left_dim, right_dim):
    return lax.dot_general(
        left, right, (((left_dim,), (right_dim,)), ((), ())), preferred_element_type=jnp.float32
    )


def head_part(block, head):
    lane = lax.broadcasted_iota(jnp.int32, block.shape, 1)
    mine = (lane >= HEAD_DIM) if head else (lane < HEAD_DIM)
    return jnp.where(mine, block, jnp.zeros_like(block))


def forward_kernel(table_ref, q_ref, k_ref, v_ref, out_ref, probs_ref, scores_ref):
    rows = q_ref.shape[0]
    length = k_ref.shape[0]
    blocks = length // rows
    halves = []
    for head in range(2):
        query = head_part(q_ref[...], head)
        peak = None
        for block in range(blocks):
            keys = k_ref[block * rows : (block + 1) * rows, :]
            start = length - (block + 1) * rows
            window = table_ref[0, head : head + 1, start : start + 2 * rows]
            spread = pltpu.roll(
                jnp.broadcast_to(window, (rows, 2 * rows)),
                rows + 1,
                1,
                stride=1,
                stride_axis=0,
            )[:, :rows]
            scores = lane_dot(keys, query, 1, 1) * SCORE_SCALE + spread
            scores_ref[block * rows : (block + 1) * rows, :] = scores
            block_peak = jnp.max(scores, axis=0, keepdims=True)
            peak = block_peak if peak is None else jnp.maximum(peak, block_peak)
        total = jnp.zeros((1, rows), jnp.float32)
        for block in range(blocks):
            part = slice(block * rows, (block + 1) * rows)
            powers = jnp.exp(scores_ref[part, :] - peak)
            scores_ref[part, :] = powers
            total = total + jnp.sum(powers, axis=0, keepdims=True)
        inverse = 1.0 / total
        result = jnp.zeros((rows, PAIR), jnp.float32)
        for block in range(blocks):
            part = slice(block * rows, (block + 1) * rows)
            probs = (scores_ref[part, :] * inverse).astype(jnp.bfloat16)
            probs_ref[head, part, :] = probs
            result = result + lane_dot(probs, v_ref[part, :], 0, 0)
        halves.append(result)
    lane = lax.broadcasted_iota(jnp.int32, (rows, PAIR), 1)
    out_ref[...] = jnp.where(lane < HEAD_DIM, halves[0], halves[1]).astype(out_ref.dtype)


def forward_attention(table, queries, keys_values):
    rows = queries.shape[0]
    length = keys_values.shape[0]
    return pl.pallas_call(
        forward_kernel,
        grid=(PAIRS,),
        in_specs=[
            pl.BlockSpec((1, 8, table.shape[2]), lambda p: (p, 0, 0)),
            pl.BlockSpec((rows, PAIR), lambda p: (0, p)),
            pl.BlockSpec((length, PAIR), lambda p: (0, p)),
            pl.BlockSpec((length, PAIR), lambda p: (0, p + PAIRS)),
        ],
        out_specs=[
            pl.BlockSpec((rows, PAIR), lambda p: (0, p)),
            pl.BlockSpec((2, length, rows), lambda p: (p, 0, 0)),
        ],
        out_shape=[
            jax.ShapeDtypeStruct((rows, D), jnp.bfloat16),
            jax.ShapeDtypeStruct((HEADS, length, rows), jnp.bfloat16),
        ],
        scratch_shapes=[pltpu.VMEM((length, rows), jnp.float32)],
        compiler_params=pltpu.CompilerParams(vmem_limit_bytes=28 * 1024 * 1024),
        cost_estimate=pl.CostEstimate(
            flops=8 * HEADS * rows * length * HEAD_DIM,
            bytes_accessed=2 * HEADS * rows * length + 4 * length * D,
            transcendentals=HEADS * rows * length,
        ),
    )(table, queries, keys_values, keys_values)


def backward_kernel(q_ref, g_ref, k_ref, v_ref, probs_ref, gq_ref, gkv_ref, diag_ref, dp_ref):
    rows = q_ref.shape[0]
    length = k_ref.shape[0]
    blocks = length // rows
    lane_row = lax.broadcasted_iota(jnp.int32, (rows, PAIR), 1)
    query_halves = []
    queries = [head_part(q_ref[...], head) for head in range(2)]
    grads = [head_part(g_ref[...], head) for head in range(2)]
    deltas = []
    for head in range(2):
        delta = jnp.zeros((1, rows), jnp.float32)
        for block in range(blocks):
            part = slice(block * rows, (block + 1) * rows)
            grad_probs = lane_dot(v_ref[part, :], grads[head], 1, 1)
            dp_ref[head, part, :] = grad_probs
            delta = delta + jnp.sum(
                grad_probs * probs_ref[head, part, :].astype(jnp.float32), axis=0, keepdims=True
            )
        deltas.append(delta)
    diag_ref[...] = jnp.zeros_like(diag_ref)
    totals = [jnp.zeros((rows, PAIR), jnp.float32) for head in range(2)]
    for block in range(blocks):
        part = slice(block * rows, (block + 1) * rows)
        start = length - (block + 1) * rows
        grad_keys = jnp.zeros((rows, PAIR), jnp.float32)
        grad_values = jnp.zeros((rows, PAIR), jnp.float32)
        for head in range(2):
            probs = probs_ref[head, part, :]
            grad_scores = probs.astype(jnp.float32) * (dp_ref[head, part, :] - deltas[head])
            low = grad_scores.astype(jnp.bfloat16)
            grad_keys = grad_keys + lane_dot(low, queries[head], 1, 0)
            grad_values = grad_values + lane_dot(probs, grads[head], 1, 0)
            totals[head] = totals[head] + lane_dot(low, k_ref[part, :], 0, 0)
            folded = jnp.zeros((8, 2 * rows), jnp.float32)
            for group in range(rows // 8):
                piece = grad_scores[8 * group : 8 * group + 8, :]
                wide = jnp.concatenate([piece, jnp.zeros_like(piece)], axis=1)
                folded = folded + pltpu.roll(wide, rows - 8 - 8 * group, 1)
            line = jnp.zeros((1, 2 * rows), jnp.float32)
            for sub in range(8):
                row = folded[sub : sub + 1, :]
                line = line + (pltpu.roll(row, 7 - sub, 1) if sub < 7 else row)
            diag_ref[0, head : head + 1, start : start + 2 * rows] += line
        gkv_ref[0, part, :] = (grad_keys * SCORE_SCALE).astype(gkv_ref.dtype)
        gkv_ref[1, part, :] = grad_values.astype(gkv_ref.dtype)
    gq_ref[...] = (jnp.where(lane_row < HEAD_DIM, totals[0], totals[1]) * SCORE_SCALE).astype(
        gq_ref.dtype
    )


def backward_attention(queries, grads, keys_values, probs):
    rows = queries.shape[0]
    length = keys_values.shape[0]
    span = length + rows
    return pl.pallas_call(
        backward_kernel,
        grid=(PAIRS,),
        in_specs=[
            pl.BlockSpec((rows, PAIR), lambda p: (0, p)),
            pl.BlockSpec((rows, PAIR), lambda p: (0, p)),
            pl.BlockSpec((length, PAIR), lambda p: (0, p)),
            pl.BlockSpec((length, PAIR), lambda p: (0, p + PAIRS)),
            pl.BlockSpec((2, length, rows), lambda p: (p, 0, 0)),
        ],
        out_specs=[
            pl.BlockSpec((rows, PAIR), lambda p: (0, p)),
            pl.BlockSpec((2, length, PAIR), lambda p: (0, 0, p)),
            pl.BlockSpec((1, 8, span), lambda p: (p, 0, 0)),
        ],
        out_shape=[
            jax.ShapeDtypeStruct((rows, D), jnp.bfloat16),
            jax.ShapeDtypeStruct((2, length, D), jnp.bfloat16),
            jax.ShapeDtypeStruct((PAIRS, 8, span), jnp.float32),
        ],
        scratch_shapes=[pltpu.VMEM((2, length, rows), jnp.float32)],
        compiler_params=pltpu.CompilerParams(vmem_limit_bytes=28 * 1024 * 1024),
        cost_estimate=pl.CostEstimate(
            flops=20 * HEADS * rows * length * HEAD_DIM,
            bytes_accessed=2 * HEADS * rows * length + 8 * length * D,
            transcendentals=0,
        ),
    )(queries, grads, keys_values, keys_values, probs)


def gelu_both(pre):
    inner = jnp.tanh(GELU_ROOT * (pre + GELU_CUBE * pre * pre * pre))
    half = 0.5 * (1.0 + inner)
    slope = half + 0.5 * pre * (1.0 - inner * inner) * (
        GELU_ROOT * (1.0 + 3.0 * GELU_CUBE * pre * pre)
    )
    return (pre * half, slope)


def expert_hidden(rows, weight_in, weight_out):
    pre = jnp.dot(rows[:, :D], weight_in, preferred_element_type=jnp.float32)
    grad_act = lane_dot(rows[:, D:], weight_out, 1, 1)
    value, slope = gelu_both(pre)
    return (value.astype(jnp.bfloat16), (grad_act * slope).astype(jnp.bfloat16))


def body(
    tokens,
    norm1_gain,
    w_qkv,
    w_out,
    bias_table,
    norm2_gain,
    router,
    expert_in,
    expert_out,
    route,
    slot,
    cotangent,
):
    seqs_here, rows_seq, width = tokens.shape
    contexts = lax.axis_size("context")
    ctx_index = lax.axis_index("context")
    experts_total = router.shape[1]
    tok_rows = seqs_here * rows_seq
    capacity = max(2, 5 * tok_rows // (4 * experts_total))
    query_start = ctx_index * rows_seq
    length = rows_seq * contexts
    weight_in = expert_in[0]
    weight_out = expert_out[0]
    inputs = tokens.astype(jnp.float32).reshape(tok_rows, D)
    grad_out = cotangent.astype(jnp.float32).reshape(tok_rows, D)
    inv_one = lax.rsqrt(jnp.mean(inputs * inputs, axis=1, keepdims=True) + EPSILON)
    normed_one = (inputs * inv_one * norm1_gain).astype(jnp.bfloat16)
    keys_values = lax.all_gather(
        jnp.dot(normed_one, w_qkv[:, D:], preferred_element_type=jnp.float32).astype(jnp.bfloat16),
        "context",
        axis=0,
        tiled=True,
    )
    queries = jnp.dot(normed_one, w_qkv[:, :D], preferred_element_type=jnp.float32).astype(
        jnp.bfloat16
    )
    span = length + rows_seq
    relative = (length - 1 - query_start) - jnp.arange(span, dtype=jnp.int32)
    line_onehot = (
        bucket_index(relative)[None, :] == jnp.arange(BUCKETS, dtype=jnp.int32)[:, None]
    ).astype(jnp.float32)
    line_table = lax.dot_general(
        bias_table, line_onehot, (((0,), (0,)), ((), ())), precision=HIGHEST
    ).reshape(PAIRS, 2, span)
    line_table = jnp.pad(line_table, ((0, 0), (0, 6), (0, 0)))
    attn_low, probs = forward_attention(line_table, queries, keys_values)
    normed_all = lax.all_gather(normed_one, "expert", axis=0, tiled=True)
    attn_all = lax.all_gather(attn_low, "expert", axis=0, tiled=True)
    branch = jnp.dot(attn_low, w_out, preferred_element_type=jnp.float32)
    hidden_sum = inputs + branch
    inv_two = lax.rsqrt(jnp.mean(hidden_sum * hidden_sum, axis=1, keepdims=True) + EPSILON)
    normed_two = hidden_sum * inv_two * norm2_gain
    gates_all = jax.nn.softmax(jnp.dot(normed_two, router, precision=HIGHEST), axis=1)
    routes = route.reshape(tok_rows)
    slots = slot.reshape(tok_rows)
    chosen = (routes[:, None] == jnp.arange(experts_total, dtype=jnp.int32)[None, :]).astype(
        jnp.float32
    )
    gate = jnp.sum(gates_all * chosen, axis=1)
    flat_index = jnp.where(slots >= 0, routes * capacity + slots, -1)
    places = (
        flat_index[:, None] == jnp.arange(experts_total * capacity, dtype=jnp.int32)[None, :]
    ).astype(jnp.bfloat16)
    both_rows = jnp.concatenate(
        [normed_two.astype(jnp.bfloat16), (gate[:, None] * grad_out).astype(jnp.bfloat16)], axis=1
    )
    send_rows = lane_dot(places, both_rows, 0, 0).astype(jnp.bfloat16)
    received = lax.all_to_all(
        send_rows.reshape(experts_total, capacity, 2 * D),
        "expert",
        split_axis=0,
        concat_axis=0,
        tiled=True,
    ).reshape(experts_total * capacity, 2 * D)
    activated, grad_pre = expert_hidden(received, weight_in, weight_out)
    produced = jnp.dot(activated, weight_out, preferred_element_type=jnp.float32)
    grad_sent = lane_dot(grad_pre, weight_in, 1, 1)
    answer = jnp.concatenate([produced, grad_sent], axis=1).astype(jnp.bfloat16)
    answer = lax.all_to_all(
        answer.reshape(experts_total, capacity, 2 * D),
        "expert",
        split_axis=0,
        concat_axis=0,
        tiled=True,
    ).reshape(experts_total * capacity, 2 * D)
    group_rows = lax.all_gather(received, ("dp", "context"), axis=0, tiled=True)
    copies = lax.axis_size("dp") * contexts
    share = weight_in.shape[1] // copies
    first = (lax.axis_index("dp") * contexts + ctx_index) * share
    slice_act, slice_pre = expert_hidden(
        group_rows,
        lax.dynamic_slice_in_dim(weight_in, first, share, axis=1),
        lax.dynamic_slice_in_dim(weight_out, first, share, axis=0),
    )
    grad_in_part = lane_dot(group_rows[:, :D], slice_pre, 0, 0)[None]
    grad_out_part = lane_dot(slice_act, group_rows[:, D:], 0, 0)[None]

    back_rows = jnp.dot(places, answer, preferred_element_type=jnp.float32)
    expert_rows = back_rows[:, :D]
    layer_rows = hidden_sum + gate[:, None] * expert_rows
    layer_out = layer_rows.astype(jnp.bfloat16).reshape(tokens.shape)
    grad_gate = jnp.sum(grad_out * expert_rows, axis=1)
    grad_probs_gate = chosen * grad_gate[:, None]
    grad_logits = gates_all * (
        grad_probs_gate - jnp.sum(gates_all * grad_probs_gate, axis=1, keepdims=True)
    )
    grad_router = jnp.dot(normed_two.T, grad_logits, precision=HIGHEST)
    grad_normed = back_rows[:, D:] + jnp.dot(grad_logits, router.T, precision=HIGHEST)
    grad_norm2, grad_from_norm = norm_back(grad_normed, hidden_sum, inv_two, norm2_gain)
    grad_hidden = grad_out + grad_from_norm
    grad_branch = grad_hidden.astype(jnp.bfloat16)
    grad_attn_low = lane_dot(grad_branch, w_out, 1, 1).astype(jnp.bfloat16)
    grad_q, key_value_terms, diagonals = backward_attention(
        queries, grad_attn_low, keys_values, probs
    )
    grad_table = lax.dot_general(
        line_onehot,
        diagonals[:, :2].reshape(HEADS, span),
        (((1,), (1,)), ((), ())),
        precision=HIGHEST,
    )
    key_value_grad = lax.psum_scatter(key_value_terms, "context", scatter_dimension=1, tiled=True)
    grad_proj = jnp.concatenate([grad_q, key_value_grad[0], key_value_grad[1]], axis=1)
    grad_normed_one = lane_dot(grad_proj, w_qkv, 1, 1)
    grad_norm1, grad_from_first = norm_back(grad_normed_one, inputs, inv_one, norm1_gain)
    input_grad = (grad_hidden + grad_from_first).astype(jnp.bfloat16).reshape(tokens.shape)

    owners = lax.axis_size("expert")
    proj_share = 3 * D // owners
    wout_share = D // owners
    columns = jnp.concatenate(
        [
            grad_proj.reshape(tok_rows, owners, proj_share),
            grad_branch.reshape(tok_rows, owners, wout_share),
        ],
        axis=2,
    )
    columns = lax.all_to_all(
        jnp.transpose(columns, (1, 0, 2)), "expert", split_axis=0, concat_axis=0, tiled=True
    ).reshape(owners * tok_rows, proj_share + wout_share)
    part = jnp.concatenate(
        [
            lane_dot(normed_all, columns[:, :proj_share], 0, 0),
            lane_dot(attn_all, columns[:, proj_share:], 0, 0),
        ],
        axis=1,
    ).astype(jnp.bfloat16)
    part = lax.psum_scatter(
        part, ("dp", "context"), scatter_dimension=0, tiled=True
    ).astype(jnp.float32)
    sum_norm1, sum_table, sum_norm2, sum_router = lax.psum(
        (grad_norm1, grad_table, grad_norm2, grad_router), ("dp", "context", "expert")
    )
    return (
        layer_out,
        input_grad,
        sum_norm1,
        part[:, :proj_share],
        part[:, proj_share:],
        sum_table,
        sum_norm2,
        sum_router,
        grad_in_part,
        grad_out_part,
    )


def solution(mesh):
    in_specs = (
        P(("dp", "expert"), "context", None),
        P(),
        P(),
        P(),
        P(),
        P(),
        P(),
        P("expert", None, None),
        P("expert", None, None),
        P(("dp", "expert"), "context"),
        P(("dp", "expert"), "context"),
        P(("dp", "expert"), "context", None),
    )
    out_specs = (
        P(("dp", "expert"), "context", None),
        P(("dp", "expert"), "context", None),
        P(),
        P(("dp", "context"), "expert"),
        P(("dp", "context"), "expert"),
        P(),
        P(),
        P(),
        P("expert", None, ("dp", "context")),
        P("expert", ("dp", "context"), None),
    )
    return jax.shard_map(body, mesh=mesh, in_specs=in_specs, out_specs=out_specs, check_vma=False)
```

```python
import jax
import jax.numpy as jnp
from jax import lax
from jax.experimental import pallas as pl
from jax.experimental.pallas import tpu as pltpu
from jax.sharding import PartitionSpec as P

D = 768
HEADS = 12
HEAD_DIM = 64
BUCKETS = 32


THRESHOLDS = (12, 16, 23, 32, 46, 64, 91)
SCORE_SCALE = 0.125
EPSILON = 1e-06
HIGHEST = lax.Precision.HIGHEST


def bucket_index(relative):
    distance = jnp.abs(relative)
    far_level = jnp.full_like(distance, 8)
    for threshold in THRESHOLDS:
        far_level = far_level + (distance >= threshold).astype(jnp.int32)
    near_far = jnp.where(distance < 8, distance, far_level)
    return near_far + 16 * (relative > 0).astype(jnp.int32)


def norm_back(grad_normed, values, inverse, gain):
    scaled_grad = grad_normed * gain
    grad_gain = jnp.sum(grad_normed * values * inverse, axis=0)
    grad_values = inverse * scaled_grad - values * inverse**3 * jnp.mean(
        scaled_grad * values, axis=1, keepdims=True
    )
    return (grad_gain, grad_values)


PAIR = 2 * HEAD_DIM
PAIRS = HEADS // 2
GELU_ROOT = 0.7978845608028654
GELU_CUBE = 0.044715


def lane_dot(left, right, left_dim, right_dim):
    return lax.dot_general(
        left, right, (((left_dim,), (right_dim,)), ((), ())), preferred_element_type=jnp.float32
    )


def head_part(block, head):
    lane = lax.broadcasted_iota(jnp.int32, block.shape, 1)
    mine = (lane >= HEAD_DIM) if head else (lane < HEAD_DIM)
    return jnp.where(mine, block, jnp.zeros_like(block))


def forward_kernel(table_ref, q_ref, k_ref, v_ref, out_ref, probs_ref, scores_ref):
    rows = q_ref.shape[0]
    length = k_ref.shape[0]
    blocks = length // rows
    halves = []
    for head in range(2):
        query = head_part(q_ref[...], head)
        peak = None
        for block in range(blocks):
            keys = k_ref[block * rows : (block + 1) * rows, :]
            start = length - (block + 1) * rows
            window = table_ref[0, head : head + 1, start : start + 2 * rows]
            spread = pltpu.roll(
                jnp.broadcast_to(window, (rows, 2 * rows)),
                rows + 1,
                1,
                stride=1,
                stride_axis=0,
            )[:, :rows]
            scores = lane_dot(keys, query, 1, 1) * SCORE_SCALE + spread
            scores_ref[block * rows : (block + 1) * rows, :] = scores
            block_peak = jnp.max(scores, axis=0, keepdims=True)
            peak = block_peak if peak is None else jnp.maximum(peak, block_peak)
        total = jnp.zeros((1, rows), jnp.float32)
        for block in range(blocks):
            part = slice(block * rows, (block + 1) * rows)
            powers = jnp.exp(scores_ref[part, :] - peak)
            scores_ref[part, :] = powers
            total = total + jnp.sum(powers, axis=0, keepdims=True)
        inverse = 1.0 / total
        result = jnp.zeros((rows, PAIR), jnp.float32)
        for block in range(blocks):
            part = slice(block * rows, (block + 1) * rows)
            probs = (scores_ref[part, :] * inverse).astype(jnp.bfloat16)
            probs_ref[head, part, :] = probs
            result = result + lane_dot(probs, v_ref[part, :], 0, 0)
        halves.append(result)
    lane = lax.broadcasted_iota(jnp.int32, (rows, PAIR), 1)
    out_ref[...] = jnp.where(lane < HEAD_DIM, halves[0], halves[1]).astype(out_ref.dtype)


def forward_attention(table, queries, keys_values):
    rows = queries.shape[0]
    length = keys_values.shape[0]
    return pl.pallas_call(
        forward_kernel,
        grid=(PAIRS,),
        in_specs=[
            pl.BlockSpec((1, 8, table.shape[2]), lambda p: (p, 0, 0)),
            pl.BlockSpec((rows, PAIR), lambda p: (0, p)),
            pl.BlockSpec((length, PAIR), lambda p: (0, p)),
            pl.BlockSpec((length, PAIR), lambda p: (0, p + PAIRS)),
        ],
        out_specs=[
            pl.BlockSpec((rows, PAIR), lambda p: (0, p)),
            pl.BlockSpec((2, length, rows), lambda p: (p, 0, 0)),
        ],
        out_shape=[
            jax.ShapeDtypeStruct((rows, D), jnp.bfloat16),
            jax.ShapeDtypeStruct((HEADS, length, rows), jnp.bfloat16),
        ],
        scratch_shapes=[pltpu.VMEM((length, rows), jnp.float32)],
        compiler_params=pltpu.CompilerParams(vmem_limit_bytes=28 * 1024 * 1024),
        cost_estimate=pl.CostEstimate(
            flops=8 * HEADS * rows * length * HEAD_DIM,
            bytes_accessed=2 * HEADS * rows * length + 4 * length * D,
            transcendentals=HEADS * rows * length,
        ),
    )(table, queries, keys_values, keys_values)


def backward_kernel(q_ref, g_ref, k_ref, v_ref, probs_ref, gq_ref, gk_ref, gv_ref, diag_ref, dp_ref):
    rows = q_ref.shape[0]
    length = k_ref.shape[0]
    blocks = length // rows
    lane_row = lax.broadcasted_iota(jnp.int32, (rows, PAIR), 1)
    query_halves = []
    queries = [head_part(q_ref[...], head) for head in range(2)]
    grads = [head_part(g_ref[...], head) for head in range(2)]
    deltas = []
    for head in range(2):
        delta = jnp.zeros((1, rows), jnp.float32)
        for block in range(blocks):
            part = slice(block * rows, (block + 1) * rows)
            grad_probs = lane_dot(v_ref[part, :], grads[head], 1, 1)
            dp_ref[head, part, :] = grad_probs
            delta = delta + jnp.sum(
                grad_probs * probs_ref[head, part, :].astype(jnp.float32), axis=0, keepdims=True
            )
        deltas.append(delta)
    diag_ref[...] = jnp.zeros_like(diag_ref)
    totals = [jnp.zeros((rows, PAIR), jnp.float32) for head in range(2)]
    for block in range(blocks):
        part = slice(block * rows, (block + 1) * rows)
        start = length - (block + 1) * rows
        grad_keys = jnp.zeros((rows, PAIR), jnp.float32)
        grad_values = jnp.zeros((rows, PAIR), jnp.float32)
        for head in range(2):
            probs = probs_ref[head, part, :]
            grad_scores = probs.astype(jnp.float32) * (dp_ref[head, part, :] - deltas[head])
            low = grad_scores.astype(jnp.bfloat16)
            grad_keys = grad_keys + lane_dot(low, queries[head], 1, 0)
            grad_values = grad_values + lane_dot(probs, grads[head], 1, 0)
            totals[head] = totals[head] + lane_dot(low, k_ref[part, :], 0, 0)
            folded = jnp.zeros((8, 2 * rows), jnp.float32)
            for group in range(rows // 8):
                piece = grad_scores[8 * group : 8 * group + 8, :]
                wide = jnp.concatenate([piece, jnp.zeros_like(piece)], axis=1)
                folded = folded + pltpu.roll(wide, rows - 8 - 8 * group, 1)
            line = jnp.zeros((1, 2 * rows), jnp.float32)
            for sub in range(8):
                row = folded[sub : sub + 1, :]
                line = line + (pltpu.roll(row, 7 - sub, 1) if sub < 7 else row)
            diag_ref[0, head : head + 1, start : start + 2 * rows] += line
        gk_ref[part, :] = (grad_keys * SCORE_SCALE).astype(gk_ref.dtype)
        gv_ref[part, :] = grad_values.astype(gv_ref.dtype)
    gq_ref[...] = (jnp.where(lane_row < HEAD_DIM, totals[0], totals[1]) * SCORE_SCALE).astype(
        gq_ref.dtype
    )


def backward_attention(queries, grads, keys_values, probs):
    rows = queries.shape[0]
    length = keys_values.shape[0]
    span = length + rows
    return pl.pallas_call(
        backward_kernel,
        grid=(PAIRS,),
        in_specs=[
            pl.BlockSpec((rows, PAIR), lambda p: (0, p)),
            pl.BlockSpec((rows, PAIR), lambda p: (0, p)),
            pl.BlockSpec((length, PAIR), lambda p: (0, p)),
            pl.BlockSpec((length, PAIR), lambda p: (0, p + PAIRS)),
            pl.BlockSpec((2, length, rows), lambda p: (p, 0, 0)),
        ],
        out_specs=[
            pl.BlockSpec((rows, PAIR), lambda p: (0, p)),
            pl.BlockSpec((length, PAIR), lambda p: (0, p)),
            pl.BlockSpec((length, PAIR), lambda p: (0, p)),
            pl.BlockSpec((1, 8, span), lambda p: (p, 0, 0)),
        ],
        out_shape=[
            jax.ShapeDtypeStruct((rows, D), jnp.bfloat16),
            jax.ShapeDtypeStruct((length, D), jnp.bfloat16),
            jax.ShapeDtypeStruct((length, D), jnp.bfloat16),
            jax.ShapeDtypeStruct((PAIRS, 8, span), jnp.float32),
        ],
        scratch_shapes=[pltpu.VMEM((2, length, rows), jnp.float32)],
        compiler_params=pltpu.CompilerParams(vmem_limit_bytes=28 * 1024 * 1024),
        cost_estimate=pl.CostEstimate(
            flops=20 * HEADS * rows * length * HEAD_DIM,
            bytes_accessed=2 * HEADS * rows * length + 8 * length * D,
            transcendentals=0,
        ),
    )(queries, grads, keys_values, keys_values, probs)


def gelu_both(pre):
    inner = jnp.tanh(GELU_ROOT * (pre + GELU_CUBE * pre * pre * pre))
    half = 0.5 * (1.0 + inner)
    slope = half + 0.5 * pre * (1.0 - inner * inner) * (
        GELU_ROOT * (1.0 + 3.0 * GELU_CUBE * pre * pre)
    )
    return (pre * half, slope)


def expert_hidden(rows, weight_in, weight_out):
    pre = jnp.dot(rows[:, :D], weight_in, preferred_element_type=jnp.float32)
    grad_act = lane_dot(rows[:, D:], weight_out, 1, 1)
    value, slope = gelu_both(pre)
    return (value.astype(jnp.bfloat16), (grad_act * slope).astype(jnp.bfloat16))


def body(
    tokens,
    norm1_gain,
    w_qkv,
    w_out,
    bias_table,
    norm2_gain,
    router,
    expert_in,
    expert_out,
    route,
    slot,
    cotangent,
):
    seqs_here, rows_seq, width = tokens.shape
    contexts = lax.axis_size("context")
    ctx_index = lax.axis_index("context")
    experts_total = router.shape[1]
    tok_rows = seqs_here * rows_seq
    capacity = max(2, 5 * tok_rows // (4 * experts_total))
    query_start = ctx_index * rows_seq
    length = rows_seq * contexts
    weight_in = expert_in[0]
    weight_out = expert_out[0]
    inputs = tokens.astype(jnp.float32).reshape(tok_rows, D)
    grad_out = cotangent.astype(jnp.float32).reshape(tok_rows, D)
    inv_one = lax.rsqrt(jnp.mean(inputs * inputs, axis=1, keepdims=True) + EPSILON)
    normed_one = (inputs * inv_one * norm1_gain).astype(jnp.bfloat16)
    normed_seq = lax.all_gather(normed_one, "context", axis=0, tiled=True)
    keys_values = jnp.dot(normed_seq, w_qkv[:, D:], preferred_element_type=jnp.float32).astype(
        jnp.bfloat16
    )
    queries = jnp.dot(normed_one, w_qkv[:, :D], preferred_element_type=jnp.float32).astype(
        jnp.bfloat16
    )
    span = length + rows_seq
    relative = (length - 1 - query_start) - jnp.arange(span, dtype=jnp.int32)
    line_onehot = (
        bucket_index(relative)[None, :] == jnp.arange(BUCKETS, dtype=jnp.int32)[:, None]
    ).astype(jnp.float32)
    line_table = lax.dot_general(
        bias_table, line_onehot, (((0,), (0,)), ((), ())), precision=HIGHEST
    ).reshape(PAIRS, 2, span)
    line_table = jnp.pad(line_table, ((0, 0), (0, 6), (0, 0)))
    attn_low, probs = forward_attention(line_table, queries, keys_values)
    branch = jnp.dot(attn_low, w_out, preferred_element_type=jnp.float32)
    hidden_sum = inputs + branch
    inv_two = lax.rsqrt(jnp.mean(hidden_sum * hidden_sum, axis=1, keepdims=True) + EPSILON)
    normed_two = hidden_sum * inv_two * norm2_gain
    gates_all = jax.nn.softmax(jnp.dot(normed_two, router, precision=HIGHEST), axis=1)
    routes = route.reshape(tok_rows)
    slots = slot.reshape(tok_rows)
    chosen = (routes[:, None] == jnp.arange(experts_total, dtype=jnp.int32)[None, :]).astype(
        jnp.float32
    )
    gate = jnp.sum(gates_all * chosen, axis=1)
    flat_index = jnp.where(slots >= 0, routes * capacity + slots, -1)
    places = (
        flat_index[:, None] == jnp.arange(experts_total * capacity, dtype=jnp.int32)[None, :]
    ).astype(jnp.bfloat16)
    both_rows = jnp.concatenate(
        [normed_two.astype(jnp.bfloat16), (gate[:, None] * grad_out).astype(jnp.bfloat16)], axis=1
    )
    send_rows = lane_dot(places, both_rows, 0, 0).astype(jnp.bfloat16)
    received = lax.all_to_all(
        send_rows.reshape(experts_total, capacity, 2 * D),
        "expert",
        split_axis=0,
        concat_axis=0,
        tiled=True,
    ).reshape(experts_total * capacity, 2 * D)
    group_rows = lax.all_gather(received, ("dp", "context"), axis=0, tiled=True)
    activated, grad_pre = expert_hidden(received, weight_in, weight_out)
    produced = jnp.dot(activated, weight_out, preferred_element_type=jnp.float32)
    grad_sent = lane_dot(grad_pre, weight_in, 1, 1)
    answer = jnp.concatenate([produced, grad_sent], axis=1).astype(jnp.bfloat16)
    answer = lax.all_to_all(
        answer.reshape(experts_total, capacity, 2 * D),
        "expert",
        split_axis=0,
        concat_axis=0,
        tiled=True,
    ).reshape(experts_total * capacity, 2 * D)
    back_rows = jnp.dot(places, answer, preferred_element_type=jnp.float32)
    expert_rows = back_rows[:, :D]
    layer_rows = hidden_sum + gate[:, None] * expert_rows
    layer_out = layer_rows.astype(jnp.bfloat16).reshape(tokens.shape)
    grad_gate = jnp.sum(grad_out * expert_rows, axis=1)
    grad_probs_gate = chosen * grad_gate[:, None]
    grad_logits = gates_all * (
        grad_probs_gate - jnp.sum(gates_all * grad_probs_gate, axis=1, keepdims=True)
    )
    grad_router = jnp.dot(normed_two.T, grad_logits, precision=HIGHEST)
    grad_normed = back_rows[:, D:] + jnp.dot(grad_logits, router.T, precision=HIGHEST)
    grad_norm2, grad_from_norm = norm_back(grad_normed, hidden_sum, inv_two, norm2_gain)
    grad_hidden = grad_out + grad_from_norm
    grad_branch = grad_hidden.astype(jnp.bfloat16)
    grad_attn_low = lane_dot(grad_branch, w_out, 1, 1).astype(jnp.bfloat16)
    grad_attn_low, group_rows = lax.optimization_barrier((grad_attn_low, group_rows))
    grad_wout = lane_dot(attn_low, grad_branch, 0, 0).astype(jnp.bfloat16)
    grad_q, key_terms, value_terms, diagonals = backward_attention(
        queries, grad_attn_low, keys_values, probs
    )
    grad_table = lax.dot_general(
        line_onehot,
        diagonals[:, :2].reshape(HEADS, span),
        (((1,), (1,)), ((), ())),
        precision=HIGHEST,
    )
    normed_terms = lane_dot(key_terms, w_qkv[:, D : 2 * D], 1, 1) + lane_dot(
        value_terms, w_qkv[:, 2 * D :], 1, 1
    )
    normed_terms, grad_q, key_terms, value_terms = lax.optimization_barrier(
        (normed_terms.astype(jnp.bfloat16), grad_q, key_terms, value_terms)
    )
    copies = lax.axis_size("dp") * contexts
    share = weight_in.shape[1] // copies
    first = (lax.axis_index("dp") * contexts + ctx_index) * share
    slice_act, slice_pre = expert_hidden(
        group_rows,
        lax.dynamic_slice_in_dim(weight_in, first, share, axis=1),
        lax.dynamic_slice_in_dim(weight_out, first, share, axis=0),
    )
    summed_terms = lax.psum_scatter(normed_terms, "context", scatter_dimension=0, tiled=True)
    summed_terms, slice_act, slice_pre = lax.optimization_barrier(
        (summed_terms, slice_act, slice_pre)
    )
    grad_normed_one = summed_terms.astype(jnp.float32) + lane_dot(grad_q, w_qkv[:, :D], 1, 1)
    grad_norm1, grad_from_first = norm_back(grad_normed_one, inputs, inv_one, norm1_gain)
    input_grad = (grad_hidden + grad_from_first).astype(jnp.bfloat16).reshape(tokens.shape)

    grad_in_part = lane_dot(group_rows[:, :D], slice_pre, 0, 0)[None]
    grad_out_part = lane_dot(slice_act, group_rows[:, D:], 0, 0)[None]

    owners = lax.axis_size("expert")
    proj_share = 3 * D // owners
    grad_both = jnp.concatenate(
        [
            lane_dot(normed_one, grad_q, 0, 0).astype(jnp.bfloat16),
            lane_dot(normed_seq, key_terms, 0, 0).astype(jnp.bfloat16),
            lane_dot(normed_seq, value_terms, 0, 0).astype(jnp.bfloat16),
            grad_wout,
        ],
        axis=1,
    )
    part_both = lax.psum_scatter(grad_both, ("dp", "context"), scatter_dimension=0, tiled=True)
    part_qkv, part_wout = part_both[:, : 3 * D], part_both[:, 3 * D :]
    rows_here = part_both.shape[0]
    part = jnp.concatenate(
        [part_qkv.reshape(rows_here, owners, -1), part_wout.reshape(rows_here, owners, -1)], axis=2
    )
    part = lax.psum_scatter(
        jnp.transpose(part, (1, 0, 2)), "expert", scatter_dimension=0, tiled=True
    )[0].astype(jnp.float32)
    sum_norm1, sum_table, sum_norm2, sum_router = lax.psum(
        (grad_norm1, grad_table, grad_norm2, grad_router), ("dp", "context", "expert")
    )
    return (
        layer_out,
        input_grad,
        sum_norm1,
        part[:, :proj_share],
        part[:, proj_share:],
        sum_table,
        sum_norm2,
        sum_router,
        grad_in_part,
        grad_out_part,
    )


def solution(mesh):
    in_specs = (
        P(("dp", "expert"), "context", None),
        P(),
        P(),
        P(),
        P(),
        P(),
        P(),
        P("expert", None, None),
        P("expert", None, None),
        P(("dp", "expert"), "context"),
        P(("dp", "expert"), "context"),
        P(("dp", "expert"), "context", None),
    )
    out_specs = (
        P(("dp", "expert"), "context", None),
        P(("dp", "expert"), "context", None),
        P(),
        P(("dp", "context"), "expert"),
        P(("dp", "context"), "expert"),
        P(),
        P(),
        P(),
        P("expert", None, ("dp", "context")),
        P("expert", ("dp", "context"), None),
    )
    return jax.shard_map(body, mesh=mesh, in_specs=in_specs, out_specs=out_specs, check_vma=False)
```

```python
import jax
import jax.numpy as jnp
from jax import lax
from jax.experimental import pallas as pl
from jax.experimental.pallas import tpu as pltpu
from jax.sharding import PartitionSpec as P

D = 768
HEADS = 12
HEAD_DIM = 64
BUCKETS = 32


THRESHOLDS = (12, 16, 23, 32, 46, 64, 91)
SCORE_SCALE = 0.125
EPSILON = 1e-06
HIGHEST = lax.Precision.HIGHEST


def bucket_index(relative):
    distance = jnp.abs(relative)
    far_level = jnp.full_like(distance, 8)
    for threshold in THRESHOLDS:
        far_level = far_level + (distance >= threshold).astype(jnp.int32)
    near_far = jnp.where(distance < 8, distance, far_level)
    return near_far + 16 * (relative > 0).astype(jnp.int32)


def norm_back(grad_normed, values, inverse, gain):
    scaled_grad = grad_normed * gain
    grad_gain = jnp.sum(grad_normed * values * inverse, axis=0)
    grad_values = inverse * scaled_grad - values * inverse**3 * jnp.mean(
        scaled_grad * values, axis=1, keepdims=True
    )
    return (grad_gain, grad_values)


PAIR = 2 * HEAD_DIM
PAIRS = HEADS // 2
GELU_ROOT = 0.7978845608028654
GELU_CUBE = 0.044715


def lane_dot(left, right, left_dim, right_dim):
    return lax.dot_general(
        left, right, (((left_dim,), (right_dim,)), ((), ())), preferred_element_type=jnp.float32
    )


def head_part(block, head):
    lane = lax.broadcasted_iota(jnp.int32, block.shape, 1)
    mine = (lane >= HEAD_DIM) if head else (lane < HEAD_DIM)
    return jnp.where(mine, block, jnp.zeros_like(block))


def forward_kernel(table_ref, q_ref, k_ref, v_ref, out_ref, probs_ref, scores_ref):
    rows = q_ref.shape[0]
    length = k_ref.shape[0]
    blocks = length // rows
    halves = []
    for head in range(2):
        query = head_part(q_ref[...], head)
        peak = None
        for block in range(blocks):
            keys = k_ref[block * rows : (block + 1) * rows, :]
            start = length - (block + 1) * rows
            window = table_ref[0, head : head + 1, start : start + 2 * rows]
            spread = pltpu.roll(
                jnp.broadcast_to(window, (rows, 2 * rows)),
                rows + 1,
                1,
                stride=1,
                stride_axis=0,
            )[:, :rows]
            scores = lane_dot(keys, query, 1, 1) * SCORE_SCALE + spread
            scores_ref[block * rows : (block + 1) * rows, :] = scores
            block_peak = jnp.max(scores, axis=0, keepdims=True)
            peak = block_peak if peak is None else jnp.maximum(peak, block_peak)
        total = jnp.zeros((1, rows), jnp.float32)
        for block in range(blocks):
            part = slice(block * rows, (block + 1) * rows)
            powers = jnp.exp(scores_ref[part, :] - peak)
            scores_ref[part, :] = powers
            total = total + jnp.sum(powers, axis=0, keepdims=True)
        inverse = 1.0 / total
        result = jnp.zeros((rows, PAIR), jnp.float32)
        for block in range(blocks):
            part = slice(block * rows, (block + 1) * rows)
            probs = (scores_ref[part, :] * inverse).astype(jnp.bfloat16)
            probs_ref[head, part, :] = probs
            result = result + lane_dot(probs, v_ref[part, :], 0, 0)
        halves.append(result)
    lane = lax.broadcasted_iota(jnp.int32, (rows, PAIR), 1)
    out_ref[...] = jnp.where(lane < HEAD_DIM, halves[0], halves[1]).astype(out_ref.dtype)


def forward_attention(table, queries, keys_values):
    rows = queries.shape[0]
    length = keys_values.shape[0]
    return pl.pallas_call(
        forward_kernel,
        grid=(PAIRS,),
        in_specs=[
            pl.BlockSpec((1, 8, table.shape[2]), lambda p: (p, 0, 0)),
            pl.BlockSpec((rows, PAIR), lambda p: (0, p)),
            pl.BlockSpec((length, PAIR), lambda p: (0, p)),
            pl.BlockSpec((length, PAIR), lambda p: (0, p + PAIRS)),
        ],
        out_specs=[
            pl.BlockSpec((rows, PAIR), lambda p: (0, p)),
            pl.BlockSpec((2, length, rows), lambda p: (p, 0, 0)),
        ],
        out_shape=[
            jax.ShapeDtypeStruct((rows, D), jnp.bfloat16),
            jax.ShapeDtypeStruct((HEADS, length, rows), jnp.bfloat16),
        ],
        scratch_shapes=[pltpu.VMEM((length, rows), jnp.float32)],
        compiler_params=pltpu.CompilerParams(vmem_limit_bytes=28 * 1024 * 1024),
        cost_estimate=pl.CostEstimate(
            flops=8 * HEADS * rows * length * HEAD_DIM,
            bytes_accessed=2 * HEADS * rows * length + 4 * length * D,
            transcendentals=HEADS * rows * length,
        ),
    )(table, queries, keys_values, keys_values)


def backward_kernel(q_ref, g_ref, k_ref, v_ref, probs_ref, gq_ref, gk_ref, gv_ref, diag_ref, dp_ref):
    rows = q_ref.shape[0]
    length = k_ref.shape[0]
    blocks = length // rows
    lane_row = lax.broadcasted_iota(jnp.int32, (rows, PAIR), 1)
    query_halves = []
    queries = [head_part(q_ref[...], head) for head in range(2)]
    grads = [head_part(g_ref[...], head) for head in range(2)]
    deltas = []
    for head in range(2):
        delta = jnp.zeros((1, rows), jnp.float32)
        for block in range(blocks):
            part = slice(block * rows, (block + 1) * rows)
            grad_probs = lane_dot(v_ref[part, :], grads[head], 1, 1)
            dp_ref[head, part, :] = grad_probs
            delta = delta + jnp.sum(
                grad_probs * probs_ref[head, part, :].astype(jnp.float32), axis=0, keepdims=True
            )
        deltas.append(delta)
    diag_ref[...] = jnp.zeros_like(diag_ref)
    totals = [jnp.zeros((rows, PAIR), jnp.float32) for head in range(2)]
    for block in range(blocks):
        part = slice(block * rows, (block + 1) * rows)
        start = length - (block + 1) * rows
        grad_keys = jnp.zeros((rows, PAIR), jnp.float32)
        grad_values = jnp.zeros((rows, PAIR), jnp.float32)
        for head in range(2):
            probs = probs_ref[head, part, :]
            grad_scores = probs.astype(jnp.float32) * (dp_ref[head, part, :] - deltas[head])
            low = grad_scores.astype(jnp.bfloat16)
            grad_keys = grad_keys + lane_dot(low, queries[head], 1, 0)
            grad_values = grad_values + lane_dot(probs, grads[head], 1, 0)
            totals[head] = totals[head] + lane_dot(low, k_ref[part, :], 0, 0)
            folded = jnp.zeros((8, 2 * rows), jnp.float32)
            for group in range(rows // 8):
                piece = grad_scores[8 * group : 8 * group + 8, :]
                wide = jnp.concatenate([piece, jnp.zeros_like(piece)], axis=1)
                folded = folded + pltpu.roll(wide, rows - 8 - 8 * group, 1)
            line = jnp.zeros((1, 2 * rows), jnp.float32)
            for sub in range(8):
                row = folded[sub : sub + 1, :]
                line = line + (pltpu.roll(row, 7 - sub, 1) if sub < 7 else row)
            diag_ref[0, head : head + 1, start : start + 2 * rows] += line
        gk_ref[part, :] = (grad_keys * SCORE_SCALE).astype(gk_ref.dtype)
        gv_ref[part, :] = grad_values.astype(gv_ref.dtype)
    gq_ref[...] = (jnp.where(lane_row < HEAD_DIM, totals[0], totals[1]) * SCORE_SCALE).astype(
        gq_ref.dtype
    )


def backward_attention(queries, grads, keys_values, probs):
    rows = queries.shape[0]
    length = keys_values.shape[0]
    span = length + rows
    return pl.pallas_call(
        backward_kernel,
        grid=(PAIRS,),
        in_specs=[
            pl.BlockSpec((rows, PAIR), lambda p: (0, p)),
            pl.BlockSpec((rows, PAIR), lambda p: (0, p)),
            pl.BlockSpec((length, PAIR), lambda p: (0, p)),
            pl.BlockSpec((length, PAIR), lambda p: (0, p + PAIRS)),
            pl.BlockSpec((2, length, rows), lambda p: (p, 0, 0)),
        ],
        out_specs=[
            pl.BlockSpec((rows, PAIR), lambda p: (0, p)),
            pl.BlockSpec((length, PAIR), lambda p: (0, p)),
            pl.BlockSpec((length, PAIR), lambda p: (0, p)),
            pl.BlockSpec((1, 8, span), lambda p: (p, 0, 0)),
        ],
        out_shape=[
            jax.ShapeDtypeStruct((rows, D), jnp.bfloat16),
            jax.ShapeDtypeStruct((length, D), jnp.bfloat16),
            jax.ShapeDtypeStruct((length, D), jnp.bfloat16),
            jax.ShapeDtypeStruct((PAIRS, 8, span), jnp.float32),
        ],
        scratch_shapes=[pltpu.VMEM((2, length, rows), jnp.float32)],
        compiler_params=pltpu.CompilerParams(vmem_limit_bytes=28 * 1024 * 1024),
        cost_estimate=pl.CostEstimate(
            flops=20 * HEADS * rows * length * HEAD_DIM,
            bytes_accessed=2 * HEADS * rows * length + 8 * length * D,
            transcendentals=0,
        ),
    )(queries, grads, keys_values, keys_values, probs)


def gelu_both(pre):
    inner = jnp.tanh(GELU_ROOT * (pre + GELU_CUBE * pre * pre * pre))
    half = 0.5 * (1.0 + inner)
    slope = half + 0.5 * pre * (1.0 - inner * inner) * (
        GELU_ROOT * (1.0 + 3.0 * GELU_CUBE * pre * pre)
    )
    return (pre * half, slope)


def expert_hidden(rows, weight_in, weight_out):
    pre = jnp.dot(rows[:, :D], weight_in, preferred_element_type=jnp.float32)
    grad_act = lane_dot(rows[:, D:], weight_out, 1, 1)
    value, slope = gelu_both(pre)
    return (value.astype(jnp.bfloat16), (grad_act * slope).astype(jnp.bfloat16))


def body(
    tokens,
    norm1_gain,
    w_qkv,
    w_out,
    bias_table,
    norm2_gain,
    router,
    expert_in,
    expert_out,
    route,
    slot,
    cotangent,
):
    seqs_here, rows_seq, width = tokens.shape
    contexts = lax.axis_size("context")
    ctx_index = lax.axis_index("context")
    experts_total = router.shape[1]
    tok_rows = seqs_here * rows_seq
    capacity = max(2, 5 * tok_rows // (4 * experts_total))
    query_start = ctx_index * rows_seq
    length = rows_seq * contexts
    weight_in = expert_in[0]
    weight_out = expert_out[0]
    inputs = tokens.astype(jnp.float32).reshape(tok_rows, D)
    grad_out = cotangent.astype(jnp.float32).reshape(tok_rows, D)
    inv_one = lax.rsqrt(jnp.mean(inputs * inputs, axis=1, keepdims=True) + EPSILON)
    normed_one = (inputs * inv_one * norm1_gain).astype(jnp.bfloat16)
    inputs_seq = lax.all_gather(
        tokens.reshape(tok_rows, D), "context", axis=0, tiled=True
    ).astype(jnp.float32)
    unit_seq = inputs_seq * lax.rsqrt(
        jnp.mean(inputs_seq * inputs_seq, axis=1, keepdims=True) + EPSILON
    )
    normed_seq = (unit_seq * norm1_gain).astype(jnp.bfloat16)
    keys_values = jnp.dot(normed_seq, w_qkv[:, D:], preferred_element_type=jnp.float32).astype(
        jnp.bfloat16
    )
    queries = jnp.dot(normed_one, w_qkv[:, :D], preferred_element_type=jnp.float32).astype(
        jnp.bfloat16
    )
    span = length + rows_seq
    relative = (length - 1 - query_start) - jnp.arange(span, dtype=jnp.int32)
    line_onehot = (
        bucket_index(relative)[None, :] == jnp.arange(BUCKETS, dtype=jnp.int32)[:, None]
    ).astype(jnp.float32)
    line_table = lax.dot_general(
        bias_table, line_onehot, (((0,), (0,)), ((), ())), precision=HIGHEST
    ).reshape(PAIRS, 2, span)
    line_table = jnp.pad(line_table, ((0, 0), (0, 6), (0, 0)))
    attn_low, probs = forward_attention(line_table, queries, keys_values)
    branch = jnp.dot(attn_low, w_out, preferred_element_type=jnp.float32)
    hidden_sum = inputs + branch
    inv_two = lax.rsqrt(jnp.mean(hidden_sum * hidden_sum, axis=1, keepdims=True) + EPSILON)
    normed_two = hidden_sum * inv_two * norm2_gain
    gates_all = jax.nn.softmax(jnp.dot(normed_two, router, precision=HIGHEST), axis=1)
    routes = route.reshape(tok_rows)
    slots = slot.reshape(tok_rows)
    chosen = (routes[:, None] == jnp.arange(experts_total, dtype=jnp.int32)[None, :]).astype(
        jnp.float32
    )
    gate = jnp.sum(gates_all * chosen, axis=1)
    flat_index = jnp.where(slots >= 0, routes * capacity + slots, -1)
    places = (
        flat_index[:, None] == jnp.arange(experts_total * capacity, dtype=jnp.int32)[None, :]
    ).astype(jnp.bfloat16)
    both_rows = jnp.concatenate(
        [normed_two.astype(jnp.bfloat16), (gate[:, None] * grad_out).astype(jnp.bfloat16)], axis=1
    )
    send_rows = lane_dot(places, both_rows, 0, 0).astype(jnp.bfloat16)
    received = lax.all_to_all(
        send_rows.reshape(experts_total, capacity, 2 * D),
        "expert",
        split_axis=0,
        concat_axis=0,
        tiled=True,
    ).reshape(experts_total * capacity, 2 * D)
    group_rows = lax.all_gather(received, ("dp", "context"), axis=0, tiled=True)
    activated, grad_pre = expert_hidden(received, weight_in, weight_out)
    produced = jnp.dot(activated, weight_out, preferred_element_type=jnp.float32)
    grad_sent = lane_dot(grad_pre, weight_in, 1, 1)
    answer = jnp.concatenate([produced, grad_sent], axis=1).astype(jnp.bfloat16)
    answer = lax.all_to_all(
        answer.reshape(experts_total, capacity, 2 * D),
        "expert",
        split_axis=0,
        concat_axis=0,
        tiled=True,
    ).reshape(experts_total * capacity, 2 * D)
    back_rows = jnp.dot(places, answer, preferred_element_type=jnp.float32)
    expert_rows = back_rows[:, :D]
    layer_rows = hidden_sum + gate[:, None] * expert_rows
    layer_out = layer_rows.astype(jnp.bfloat16).reshape(tokens.shape)
    grad_gate = jnp.sum(grad_out * expert_rows, axis=1)
    grad_probs_gate = chosen * grad_gate[:, None]
    grad_logits = gates_all * (
        grad_probs_gate - jnp.sum(gates_all * grad_probs_gate, axis=1, keepdims=True)
    )
    grad_router = jnp.dot(normed_two.T, grad_logits, precision=HIGHEST)
    grad_normed = back_rows[:, D:] + jnp.dot(grad_logits, router.T, precision=HIGHEST)
    grad_norm2, grad_from_norm = norm_back(grad_normed, hidden_sum, inv_two, norm2_gain)
    grad_hidden = grad_out + grad_from_norm
    grad_branch = grad_hidden.astype(jnp.bfloat16)
    grad_attn_low = lane_dot(grad_branch, w_out, 1, 1).astype(jnp.bfloat16)
    grad_attn_low, group_rows = lax.optimization_barrier((grad_attn_low, group_rows))
    grad_wout = lane_dot(attn_low, grad_branch, 0, 0).astype(jnp.bfloat16)
    grad_q, key_terms, value_terms, diagonals = backward_attention(
        queries, grad_attn_low, keys_values, probs
    )
    grad_table = lax.dot_general(
        line_onehot,
        diagonals[:, :2].reshape(HEADS, span),
        (((1,), (1,)), ((), ())),
        precision=HIGHEST,
    )
    normed_terms = lane_dot(key_terms, w_qkv[:, D : 2 * D], 1, 1) + lane_dot(
        value_terms, w_qkv[:, 2 * D :], 1, 1
    )
    query_terms = lane_dot(grad_q, w_qkv[:, :D], 1, 1)
    grad_norm1 = jnp.sum(normed_terms * unit_seq, axis=0) + jnp.sum(
        query_terms * inputs * inv_one, axis=0
    )
    normed_terms, grad_q, key_terms, value_terms = lax.optimization_barrier(
        (normed_terms.astype(jnp.bfloat16), grad_q, key_terms, value_terms)
    )
    owners = lax.axis_size("expert")
    proj_share = 3 * D // owners
    grad_both = jnp.concatenate(
        [
            lane_dot(normed_one, grad_q, 0, 0).astype(jnp.bfloat16),
            lane_dot(normed_seq, key_terms, 0, 0).astype(jnp.bfloat16),
            lane_dot(normed_seq, value_terms, 0, 0).astype(jnp.bfloat16),
            grad_wout,
        ],
        axis=1,
    )
    grad_both, grad_norm1 = lax.optimization_barrier((grad_both, grad_norm1))
    sum_norm1, sum_table, sum_norm2, sum_router = lax.psum(
        (grad_norm1, grad_table, grad_norm2, grad_router), ("dp", "context", "expert")
    )
    group_rows, sum_norm1 = lax.optimization_barrier((group_rows, sum_norm1))
    copies = lax.axis_size("dp") * contexts
    share = weight_in.shape[1] // copies
    first = (lax.axis_index("dp") * contexts + ctx_index) * share
    slice_act, slice_pre = expert_hidden(
        group_rows,
        lax.dynamic_slice_in_dim(weight_in, first, share, axis=1),
        lax.dynamic_slice_in_dim(weight_out, first, share, axis=0),
    )
    summed_terms = lax.psum_scatter(normed_terms, "context", scatter_dimension=0, tiled=True)
    grad_normed_one = summed_terms.astype(jnp.float32) + query_terms
    unused_gain, grad_from_first = norm_back(grad_normed_one, inputs, inv_one, norm1_gain)
    input_grad = (grad_hidden + grad_from_first).astype(jnp.bfloat16).reshape(tokens.shape)

    grad_in_part = lane_dot(group_rows[:, :D], slice_pre, 0, 0)[None]
    grad_out_part = lane_dot(slice_act, group_rows[:, D:], 0, 0)[None]

    part_both = lax.psum_scatter(grad_both, ("dp", "context"), scatter_dimension=0, tiled=True)
    part_both, sum_norm1 = lax.optimization_barrier((part_both, sum_norm1))
    part_qkv, part_wout = part_both[:, : 3 * D], part_both[:, 3 * D :]
    rows_here = part_both.shape[0]
    part = jnp.concatenate(
        [part_qkv.reshape(rows_here, owners, -1), part_wout.reshape(rows_here, owners, -1)], axis=2
    )
    part = lax.psum_scatter(
        jnp.transpose(part, (1, 0, 2)), "expert", scatter_dimension=0, tiled=True
    )[0].astype(jnp.float32)
    return (
        layer_out,
        input_grad,
        sum_norm1,
        part[:, :proj_share],
        part[:, proj_share:],
        sum_table,
        sum_norm2,
        sum_router,
        grad_in_part,
        grad_out_part,
    )


def solution(mesh):
    in_specs = (
        P(("dp", "expert"), "context", None),
        P(),
        P(),
        P(),
        P(),
        P(),
        P(),
        P("expert", None, None),
        P("expert", None, None),
        P(("dp", "expert"), "context"),
        P(("dp", "expert"), "context"),
        P(("dp", "expert"), "context", None),
    )
    out_specs = (
        P(("dp", "expert"), "context", None),
        P(("dp", "expert"), "context", None),
        P(),
        P(("dp", "context"), "expert"),
        P(("dp", "context"), "expert"),
        P(),
        P(),
        P(),
        P("expert", None, ("dp", "context")),
        P("expert", ("dp", "context"), None),
    )
    return jax.shard_map(body, mesh=mesh, in_specs=in_specs, out_specs=out_specs, check_vma=False)
```
